32 devices in a mesh: gx: 2 (over x), gy: 4 (over y, core), ga: 4 (over z).
Axes of the slice: x: 2, y: 2, z: 4, core: 2. Of those that a mesh axis runs over, the one named last changes fastest.
Arguments:
- density: float32 [64, 768, 768], P('ga', ('gx', 'gy')), may hold values from 0.5 to 1.5
- tensor: bfloat16 [6, 64, 768, 768], P(None, 'ga', ('gx', 'gy')), may hold values from -0.29882812 to 0.29882812
- grad_u: bfloat16 [3, 64, 768, 768], P(None, 'ga', ('gx', 'gy')), may hold values from -0.099609375 to 0.099609375
- plane_rate: float32 [64], P('ga'), may hold values from 2 to 800
- cotangent: float32 [64, 768, 768], P('ga', ('gx', 'gy')), may hold values from -6 to 6
Outputs:
- new_density: float32 [64, 768, 768], P('ga', ('gx', 'gy'))
- adjoint_density: float32 [64, 768, 768], P('ga', ('gx', 'gy'))
The draws below stay inside these ranges and needn't reach their ends.
All inputs are finite; a program needn't handle non-finite values.
Results may differ from the reference program's by a relative error of at most 0.0003.
Values sent between devices are 32-bit elements; how exact they have to be, the bound alone decides.
A program may use at most 256 MiB of HBM per device.

```python
import math
import jax
import jax.numpy as jnp

NX = 768
NY = 768
NZ = 64


def level_of(own_key, dims, split, low, high):
    factor_of = 1.0
    for position, parts in split:
        steps = jax.random.uniform(jax.random.fold_in(jax.random.fold_in(own_key, 6), position), (parts,), jnp.float32, low / len(split), high / len(split))
        factor_of = factor_of * jnp.repeat(jnp.exp(steps), dims[position] // parts).reshape((-1,) + (1,) * (len(dims) - 1 - position))
    return factor_of


def bell_draw(rng, extent, width, reach, pieces=(), held_as=jnp.bfloat16):
    array = width * jax.random.normal(rng, extent, jnp.float32)
    if pieces:
        array = array * level_of(rng, extent, pieces, -0.22, 0.18)
    return jnp.clip(array, -reach, reach).astype(held_as)


def setup_inputs(seed: int = 0) -> dict:
    key_list = jax.random.split(jax.random.key(seed), 6)
    density = jnp.clip(0.5 + 1.0 * jax.random.uniform(key_list[0], (NZ, NY, NX), jnp.float32) ** level_of(key_list[0], (NZ, NY, NX), ((0, 4), (1, 8)), -0.2, 0.2), 0.5, 1.5)
    tensor = jnp.clip(jax.random.uniform(key_list[1], (6, NZ, NY, NX), jnp.float32, -0.29882812, 0.29882812) * level_of(key_list[1], (6, NZ, NY, NX), ((1, 4), (2, 8)), -0.4, 0.0), -0.29882812, 0.29882812).astype(jnp.bfloat16)
    grad_u = jnp.clip(jax.random.uniform(key_list[2], (3, NZ, NY, NX), jnp.float32, -0.099609375, 0.099609375) * level_of(key_list[2], (3, NZ, NY, NX), ((1, 4), (2, 8)), -0.4, 0.0), -0.099609375, 0.099609375).astype(jnp.bfloat16)
    plane_rate = jnp.clip(jnp.exp(math.log(800.0) - 5.9914645 * jax.random.uniform(key_list[3], (NZ,), jnp.float32) ** level_of(key_list[3], (NZ,), ((0, 4),), -0.2, 0.2)), 2.0, 800.0)
    cotangent = bell_draw(key_list[4], (NZ, NX, NY), 1.0, 6.0, ((0, 4), (1, 8)), jnp.float32)
    return {"density": density, "tensor": tensor, "grad_u": grad_u, "plane_rate": plane_rate, "cotangent": cotangent}


AXES_OF = (2, 1, 0)
ENTRY = ((0, 3, 4), (3, 1, 5), (4, 5, 2))

def central(field, along):
    return 0.5 * (jnp.roll(field, -1, along) - jnp.roll(field, 1, along))

def second(field, along):
    return jnp.roll(field, -1, along) + jnp.roll(field, 1, along) - 2.0 * field

def coupling(tensor, scales, target, source):
    entry = tensor[ENTRY[target][source]].astype(jnp.float32)
    if target == source:
        entry = entry + 1.0
    return scales[target] * scales[source] * entry

def solve_lines(field, weight, along):
    points = field.shape[along]
    spectrum = jnp.fft.rfft(field, axis=along)
    modes = jnp.arange(points // 2 + 1).astype(jnp.float32)
    factor = 1.0 + 2.0 * weight[:, 0, 0][:, None] * (1.0 - jnp.cos(2.0 * jnp.pi * modes / points))[None, :]
    if along == 2:
        factor = factor[:, None, :]
    else:
        factor = factor[:, :, None]
    return jnp.fft.irfft(spectrum / factor, n=points, axis=along).astype(field.dtype)

def reference(density, tensor, grad_u, plane_rate, cotangent):
    weight = plane_rate[:, None, None]
    rate_root = jnp.sqrt(weight)
    scales = (rate_root, rate_root, 1.0)
    drift = [grad_u[member].astype(jnp.float32) for member in range(3)]
    grads = [central(density, AXES_OF[source]) for source in range(3)]
    change = jnp.zeros_like(density)
    for target in range(3):
        flux = jnp.zeros_like(density)
        for source in range(3):
            flux = flux + coupling(tensor, scales, target, source) * (grads[source] + drift[source] * density)
        change = change + central(flux, AXES_OF[target])
    first = solve_lines(density + change - weight * second(density, 2), weight, 2)
    final = solve_lines(first - weight * second(density, 1), weight, 1)
    new_density = jnp.transpose(final, (0, 2, 1))
    adjoint_in = jnp.transpose(cotangent, (0, 2, 1))
    swept = solve_lines(adjoint_in, weight, 1)
    settled = solve_lines(swept, weight, 2)
    grads_two = [central(settled, AXES_OF[source]) for source in range(3)]
    back = jnp.zeros_like(settled)
    for target in range(3):
        pulled = jnp.zeros_like(settled)
        for source in range(3):
            pulled = pulled - coupling(tensor, scales, target, source) * grads_two[source]
        back = back - central(pulled, AXES_OF[target]) + drift[target] * pulled
    adjoint_density = settled + back - weight * second(settled, 2) - weight * second(swept, 1)
    return (new_density, adjoint_density)
```

```python
import functools
import math
import jax
import jax.numpy as jnp
from jax import lax
from jax.experimental import pallas as pl
from jax.experimental.pallas import tpu as pltpu
from jax.sharding import PartitionSpec as P

ENTRY = ((0, 3, 4), (3, 1, 5), (4, 5, 2))


def with_halo(block, sides, width):
    for axis, dim in sides:
        count = lax.axis_size(axis)
        forward = [(i, i + 1) for i in range(count - 1)]
        forward.append((count - 1, 0))
        backward = [(target, source) for source, target in forward]
        low = lax.ppermute(
            lax.slice_in_dim(block, block.shape[dim] - width, None, axis=dim), axis, forward
        )
        high = lax.ppermute(lax.slice_in_dim(block, 0, width, axis=dim), axis, backward)
        block = jnp.concatenate([low, block, high], axis=dim)
    return block


def central_last(field):
    return 0.5 * (jnp.roll(field, -1, 2) - jnp.roll(field, 1, 2))


def second_last(field):
    return jnp.roll(field, -1, 2) + jnp.roll(field, 1, 2) - 2.0 * field


def second_across(rimmed_block, member):
    return (
        rimmed_block[member, 1:-1, 2:]
        + rimmed_block[member, 1:-1, :-2]
        - 2.0 * rimmed_block[member, 1:-1, 1:-1]
    )


def hartley_matrix(points):
    counter = lax.iota(jnp.int32, points)
    product = counter[:, None] * counter[None, :] % points
    angles = 2.0 * jnp.pi / points * product.astype(jnp.float32)
    return (jnp.cos(angles) + jnp.sin(angles)) / jnp.sqrt(jnp.float32(points))


def solve_last(field, hartley_table, eigen):
    spectrum = (
        jnp.einsum("prn,nk->prk", field, hartley_table, precision=lax.Precision.HIGHEST)
        / eigen[:, None, :]
    )
    return jnp.einsum("prk,kn->prn", spectrum, hartley_table, precision=lax.Precision.HIGHEST)


def solve_swapped(field, hartley_table, eigen):
    spectrum = (
        jnp.einsum("prn,nk->prk", field, hartley_table, precision=lax.Precision.HIGHEST)
        / eigen[:, None, :]
    )
    return jnp.einsum("prk,kn->pnr", spectrum, hartley_table, precision=lax.Precision.HIGHEST)


def rimmed(stacked):
    return with_halo(stacked, ((("gx", "gy"), 2), ("ga", 1)), 1)


def gradients(rimmed_block, member, centre):
    grad_x = central_last(centre)
    grad_y = 0.5 * (rimmed_block[member, 1:-1, 2:] - rimmed_block[member, 1:-1, :-2])
    grad_z = 0.5 * (rimmed_block[member, 2:, 1:-1] - rimmed_block[member, :-2, 1:-1])
    return [grad_x, grad_y, grad_z]


def apply_tensor(tensor, rate_root, vectors):
    scales = (rate_root, rate_root, 1.0)
    results = []
    for target in range(3):
        total = jnp.zeros_like(vectors[0])
        for source in range(3):
            entry = tensor[ENTRY[target][source]].astype(jnp.float32)
            if target == source:
                entry = entry + 1.0
            total = total + scales[target] * scales[source] * entry * vectors[source]
        results.append(total)
    return results


def divergence(fluxes):
    rim_flux = with_halo(jnp.stack([fluxes[1], fluxes[2]]), ((("gx", "gy"), 2), ("ga", 1)), 1)
    across = 0.5 * (rim_flux[0, 1:-1, 2:] - rim_flux[0, 1:-1, :-2])
    planar = 0.5 * (rim_flux[1, 2:, 1:-1] - rim_flux[1, :-2, 1:-1])
    return central_last(fluxes[0]) + across + planar


def to_lines(block):
    return lax.all_to_all(block, ("gx", "gy"), split_axis=1, concat_axis=2, tiled=True)


def local_general(density, tensor, grad_u, plane_rate, cotangent):
    points = density.shape[2]
    hartley_table = hartley_matrix(points)
    modes = lax.iota(jnp.int32, points).astype(jnp.float32)
    eigen = (
        1.0 + 2.0 * plane_rate[:, None] * (1.0 - jnp.cos(2.0 * jnp.pi / points * modes))[None, :]
    )
    weight = plane_rate[:, None, None]
    rate_root = jnp.sqrt(weight)
    drift = [grad_u[member].astype(jnp.float32) for member in range(3)]
    rim_one = rimmed(density[None])
    grads = gradients(rim_one, 0, density)
    pushed = [grads[source] + drift[source] * density for source in range(3)]
    change = divergence(apply_tensor(tensor, rate_root, pushed))
    first = solve_swapped(density + change - weight * second_last(density), hartley_table, eigen)
    across = jnp.swapaxes(second_across(rim_one, 0), 1, 2)
    moved = to_lines(first - weight * across)
    new_density = solve_last(moved, hartley_table, eigen)
    swept = solve_swapped(cotangent, hartley_table, eigen)
    returned = to_lines(swept)
    settled = solve_last(returned, hartley_table, eigen)
    rim_two = rimmed(jnp.stack([settled, returned]))
    grads_two = gradients(rim_two, 0, settled)
    pulled = [-term for term in apply_tensor(tensor, rate_root, grads_two)]
    back = -divergence(pulled)
    for target in range(3):
        back = back + drift[target] * pulled[target]
    adjoint_density = (
        settled + back - weight * second_last(settled) - weight * second_across(rim_two, 1)
    )
    return (new_density, adjoint_density)


CHUNK = 256
STRIP = 16
LIMIT = 60 * 1024 * 1024


def decay_matrix(theta, kappa):
    row = lax.broadcasted_iota(jnp.int32, (CHUNK, CHUNK), 0)
    column = lax.broadcasted_iota(jnp.int32, (CHUNK, CHUNK), 1)
    distance = jnp.abs(row - column).astype(jnp.float32)
    return kappa * jnp.exp(-theta * distance)


def solve_lanes(field, par, plane):
    theta, kappa, wrap = par[plane, 2], par[plane, 3], par[plane, 4]
    matrix = decay_matrix(theta, kappa)
    count = field.shape[1] // CHUNK
    parts = [
        jnp.dot(
            field[:, CHUNK * a : CHUNK * (a + 1)],
            matrix,
            precision=lax.Precision.HIGHEST,
            preferred_element_type=jnp.float32,
        )
        for a in range(count)
    ]
    place = lax.broadcasted_iota(jnp.int32, (1, CHUNK), 1).astype(jnp.float32)
    rising = jnp.exp(-theta * (place + 1.0))
    falling = jnp.exp(-theta * (CHUNK - place))
    step = par[plane, 5]
    firsts = [part[:, :1] for part in parts]
    lasts = [part[:, CHUNK - 1 :] for part in parts]
    results = []
    for a in range(count):
        left = lasts[(a - count) % count]
        right = firsts[(a + count) % count]
        for m in range(count - 1, 0, -1):
            left = lasts[(a - m) % count] + step * left
            right = firsts[(a + m) % count] + step * right
        results.append(parts[a] + (wrap * left) * rising + (wrap * right) * falling)
    return results


def pack_plane(results, out_ref, slot, members, rows):
    whole = jnp.concatenate(results, axis=1)
    group = out_ref.shape[3] // rows
    for j in range(group):

        @pl.when(slot == j)
        def _():
            for d in range(members):
                out_ref[d, 0, :, rows * j : rows * (j + 1)] = whole[:, rows * d : rows * (d + 1)]


def lines_kernel(members, par, in_ref, out_ref):
    plane = pl.program_id(0)
    rows = in_ref.shape[1]
    group = out_ref.shape[3] // rows
    results = solve_lanes(in_ref[0], par, plane)
    pack_plane(results, out_ref, lax.rem(plane, group), members, rows)


def received_kernel(keep, par, in_ref, *outs):
    members, _, rows, lanes = in_ref.shape
    group = lanes // rows
    block = in_ref[:, 0].reshape(members * rows, lanes)
    turned = block.T
    for j in range(group):
        plane = pl.program_id(0) * group + j
        lines = turned[rows * j : rows * (j + 1)]
        results = solve_lanes(lines, par, plane)
        for a, part in enumerate(results):
            outs[0][j, :, CHUNK * a : CHUNK * (a + 1)] = part
        if keep:
            outs[1][j] = lines


def stencil_kernel(adjoint, members, par, rho, rho_z, rho_y, tensor, grad, rim_z, rim_y, *rest):
    if adjoint:
        other, other_y, out_ref, cell, flux_y, flux_z, partial = rest
    else:
        out_ref, cell, flux_y, flux_z, partial = rest
    planes, rows, lanes = rho.shape
    k = pl.program_id(0)
    now = lax.rem(k, 3)
    ring = lax.rem(k, 2)

    @pl.when(k == 0)
    def _():
        flux_z[2] = rim_z[0]

    @pl.when(k == planes)
    def _():
        flux_z[now] = rim_z[1]

    @pl.when(k < planes)
    def _():
        root = par[k, 1]
        scales = (root, root, 1.0)
        cell[8 : 8 + rows] = rho[k]
        cell[7:8] = rho_y[k, 0:1]
        cell[8 + rows : 9 + rows] = rho_y[k, 1:2]
        flux_y[7:8] = rim_y[k, 0:1]
        flux_y[8 + rows : 9 + rows] = rim_y[k, 1:2]
        before = jnp.maximum(k - 1, 0)
        after = jnp.minimum(k + 1, planes - 1)
        for s in range(rows // STRIP):
            top = STRIP * s
            span = slice(top, top + STRIP)
            centre = cell[8 + top : 8 + top + STRIP]
            low = jnp.where(k == 0, rho_z[0, span], rho[before, span])
            high = jnp.where(k == planes - 1, rho_z[1, span], rho[after, span])
            vectors = [
                0.5 * (pltpu.roll(centre, lanes - 1, 1) - pltpu.roll(centre, 1, 1)),
                0.5 * (cell[9 + top : 9 + top + STRIP] - cell[7 + top : 7 + top + STRIP]),
                0.5 * (high - low),
            ]
            drift = [grad[m, 0, span].astype(jnp.float32) for m in range(3)]
            if not adjoint:
                vectors = [vectors[m] + drift[m] * centre for m in range(3)]
            scaled = [scales[m] * vectors[m] for m in range(3)]
            entry = [tensor[m, 0, span].astype(jnp.float32) for m in range(6)]
            fluxes = []
            for target in range(3):
                total = scaled[target]
                for source in range(3):
                    total = total + entry[ENTRY[target][source]] * scaled[source]
                fluxes.append(total if target == 2 else root * total)
            change = 0.5 * (pltpu.roll(fluxes[0], lanes - 1, 1) - pltpu.roll(fluxes[0], 1, 1))
            if adjoint:
                for m in range(3):
                    change = change - drift[m] * fluxes[m]
            flux_y[8 + top : 8 + top + STRIP] = fluxes[1]
            flux_z[now, span] = fluxes[2]
            partial[ring, span] = change
        for s in range(rows // STRIP):
            top = STRIP * s
            span = slice(top, top + STRIP)
            partial[ring, span] = partial[ring, span] + 0.5 * (
                flux_y[9 + top : 9 + top + STRIP] - flux_y[7 + top : 7 + top + STRIP]
            )

    @pl.when(k > 0)
    def _():
        q = k - 1
        rate = par[q, 0]
        field, field_y = (other, other_y) if adjoint else (rho, rho_y)
        change = partial[1 - ring] + 0.5 * (flux_z[now] - flux_z[lax.rem(k + 1, 3)])
        pick = (q, slice(None), slice(None))
        if adjoint:
            centre = other[0]
            edge = other_y[q]
        else:
            centre = rho[pick]
            edge = rho_y[q]
        index = lax.broadcasted_iota(jnp.int32, (rows, lanes), 0)
        above = jnp.where(index == 0, edge[0:1], pltpu.roll(centre, 1, 0))
        below = jnp.where(index == rows - 1, edge[1:2], pltpu.roll(centre, rows - 1, 0))
        level = centre - rate * (above + below - 2.0 * centre)
        if adjoint:
            out_ref[0] = level + change
        else:
            parts = solve_lanes(change, par, q)
            parts = [
                part + level[:, CHUNK * a : CHUNK * (a + 1)] for a, part in enumerate(parts)
            ]
            group = out_ref.shape[3] // rows
            pack_plane(parts, out_ref, lax.rem(q, group), members, rows)


def exchange(low_edge, high_edge, axis):
    count = lax.axis_size(axis)
    forward = [(i, (i + 1) % count) for i in range(count)]
    backward = [(target, source) for source, target in forward]
    return lax.ppermute(high_edge, axis, forward), lax.ppermute(low_edge, axis, backward)


def rims(field):
    z_low, z_high = exchange(field[:1], field[-1:], "ga")
    y_low, y_high = exchange(field[:, :1], field[:, -1:], ("gx", "gy"))
    return jnp.concatenate([z_low, z_high], 0), jnp.concatenate([y_low, y_high], 1)


def rim_flux(target, centre, differences, tensor, grad, root, adjoint):
    scales = (root, root, 1.0)
    total = 0.0
    for source in range(3):
        vector = 0.5 * differences[source]
        if not adjoint:
            vector = vector + grad[source].astype(jnp.float32) * centre
        entry = tensor[ENTRY[target][source]].astype(jnp.float32)
        if target == source:
            entry = entry + 1.0
        total = total + scales[target] * scales[source] * entry * vector
    return total


def ends(array, axis):
    size = array.shape[axis]
    return jnp.concatenate(
        [lax.slice_in_dim(array, 0, 1, axis=axis), lax.slice_in_dim(array, size - 1, size, axis=axis)],
        axis,
    )


def flux_rims(field, field_z, field_y, tensor, grad, root, adjoint):
    def across_lanes(part):
        return jnp.roll(part, -1, 2) - jnp.roll(part, 1, 2)

    plane = ends(field, 0)
    above = jnp.concatenate([field_y[:, :1], field[:, :-1]], 1)[:: field.shape[0] - 1]
    below = jnp.concatenate([field[:, 1:], field_y[:, 1:]], 1)[:: field.shape[0] - 1]
    before = jnp.concatenate([field_z[:1], field[-2:-1]], 0)
    after = jnp.concatenate([field[1:2], field_z[1:]], 0)
    flux_z = rim_flux(
        2,
        plane,
        (across_lanes(plane), below - above, after - before),
        ends(tensor, 1),
        ends(grad, 1),
        ends(root, 0),
        adjoint,
    )
    row = ends(field, 1)
    outer = ends(field_z, 1)
    above = jnp.concatenate([field_y[:, :1], field[:, -2:-1]], 1)
    below = jnp.concatenate([field[:, 1:2], field_y[:, 1:]], 1)
    before = jnp.concatenate([outer[:1], row[:-1]], 0)
    after = jnp.concatenate([row[1:], outer[1:]], 0)
    flux_y = rim_flux(
        1,
        row,
        (across_lanes(row), below - above, after - before),
        ends(tensor, 2),
        ends(grad, 2),
        root,
        adjoint,
    )
    z_low, z_high = exchange(flux_z[:1], flux_z[1:], "ga")
    y_low, y_high = exchange(flux_y[:, :1], flux_y[:, 1:], ("gx", "gy"))
    return jnp.concatenate([z_low, z_high], 0), jnp.concatenate([y_low, y_high], 1)


def whole_block(array):
    zeros = (0,) * array.ndim
    return pl.BlockSpec(array.shape, lambda k: zeros)


def stencil(adjoint, members, group, par, root, field, tensor, grad, extra=()):
    planes, rows, lanes = field.shape
    field_z, field_y = rims(field)
    rim_z, rim_y = flux_rims(field, field_z, field_y, tensor, grad, root, adjoint)
    stream = lambda k: (0, jnp.minimum(k, planes - 1), 0, 0)
    specs = [
        pl.BlockSpec(memory_space=pltpu.SMEM),
        whole_block(field),
        whole_block(field_z),
        whole_block(field_y),
        pl.BlockSpec((6, 1, rows, lanes), stream),
        pl.BlockSpec((3, 1, rows, lanes), stream),
        whole_block(rim_z),
        whole_block(rim_y),
    ]
    args = [par, field, field_z, field_y, tensor, grad, rim_z, rim_y]
    if adjoint:
        other, other_y = extra
        specs += [
            pl.BlockSpec((1, rows, lanes), lambda k: (jnp.maximum(k - 1, 0), 0, 0)),
            whole_block(other_y),
        ]
        args += [other, other_y]
        out_shape = jax.ShapeDtypeStruct(field.shape, jnp.float32)
        out_spec = pl.BlockSpec((1, rows, lanes), lambda k: (jnp.maximum(k - 1, 0), 0, 0))
    else:
        out_shape = jax.ShapeDtypeStruct((members, planes // group, rows, group * rows), jnp.float32)
        out_spec = pl.BlockSpec(
            (members, 1, rows, group * rows), lambda k: (0, jnp.maximum(k - 1, 0) // group, 0, 0)
        )
    return pl.pallas_call(
        functools.partial(stencil_kernel, adjoint, members),
        grid=(planes + 1,),
        out_shape=out_shape,
        in_specs=specs,
        out_specs=out_spec,
        scratch_shapes=[
            pltpu.VMEM((rows + 16, lanes), jnp.float32),
            pltpu.VMEM((rows + 16, lanes), jnp.float32),
            pltpu.VMEM((3, rows, lanes), jnp.float32),
            pltpu.VMEM((2, rows, lanes), jnp.float32),
        ],
        compiler_params=pltpu.CompilerParams(vmem_limit_bytes=LIMIT),
        cost_estimate=pl.CostEstimate(
            flops=80 * field.size, bytes_accessed=32 * field.size, transcendentals=0
        ),
    )(*args)


def lines_solved(members, group, par, field):
    planes, rows, lanes = field.shape
    return pl.pallas_call(
        functools.partial(lines_kernel, members),
        grid=(planes,),
        out_shape=jax.ShapeDtypeStruct(
            (members, planes // group, rows, group * rows), jnp.float32
        ),
        in_specs=[
            pl.BlockSpec(memory_space=pltpu.SMEM),
            pl.BlockSpec((1, rows, lanes), lambda k: (k, 0, 0)),
        ],
        out_specs=pl.BlockSpec((members, 1, rows, group * rows), lambda k: (0, k // group, 0, 0)),
        compiler_params=pltpu.CompilerParams(vmem_limit_bytes=LIMIT),
        cost_estimate=pl.CostEstimate(
            flops=3072 * field.size, bytes_accessed=8 * field.size, transcendentals=0
        ),
    )(par, field)


def received_solved(keep, par, block):
    members, groups, rows, packed = block.shape
    group = packed // rows
    shape = jax.ShapeDtypeStruct((groups * group, rows, members * rows), jnp.float32)
    spec = pl.BlockSpec((group, rows, members * rows), lambda k: (k, 0, 0))
    return pl.pallas_call(
        functools.partial(received_kernel, keep),
        grid=(groups,),
        out_shape=[shape, shape] if keep else [shape],
        in_specs=[
            pl.BlockSpec(memory_space=pltpu.SMEM),
            pl.BlockSpec((members, 1, rows, packed), lambda k: (0, k, 0, 0)),
        ],
        out_specs=[spec, spec] if keep else [spec],
        compiler_params=pltpu.CompilerParams(vmem_limit_bytes=LIMIT),
        cost_estimate=pl.CostEstimate(
            flops=3072 * block.size, bytes_accessed=8 * block.size, transcendentals=0
        ),
    )(par, block)


def traded(block):
    return lax.all_to_all(block, ("gx", "gy"), split_axis=0, concat_axis=0, tiled=True)


def local(density, tensor, grad_u, plane_rate, cotangent):
    planes, rows, lanes = density.shape
    members = lanes // rows
    group = 128 // math.gcd(rows, 128)
    if rows % STRIP or planes % group or lanes % CHUNK:
        return local_general(density, tensor, grad_u, plane_rate, cotangent)
    root = jnp.sqrt(plane_rate)
    half = 0.5 / root
    theta = 2.0 * jnp.log1p(half + half * half / (1.0 + jnp.sqrt(1.0 + half * half)))
    kappa = 1.0 / jnp.sqrt(1.0 + 4.0 * plane_rate)
    wrap = 1.0 / (1.0 - jnp.exp(-theta * lanes))
    step = jnp.exp(-theta * CHUNK)
    par = jnp.stack([plane_rate, root, theta, kappa, wrap, step], 1)
    root = root[:, None, None]
    swept = traded(lines_solved(members, group, par, cotangent))
    packed = stencil(False, members, group, par, root, density, tensor, grad_u)
    packed, swept = lax.optimization_barrier((packed, swept))
    moved = traded(packed)
    settled, returned = received_solved(True, par, swept)
    low, high = exchange(returned[:, :1], returned[:, -1:], ("gx", "gy"))
    returned_y = jnp.concatenate([low, high], 1)
    adjoint_density = stencil(
        True, members, group, par, root, settled, tensor, grad_u, (returned, returned_y)
    )
    moved, adjoint_density = lax.optimization_barrier((moved, adjoint_density))
    (new_density,) = received_solved(False, par, moved)
    return (new_density, adjoint_density)


def solution(mesh):
    placed = (
        P("ga", ("gx", "gy"), None),
        P(None, "ga", ("gx", "gy"), None),
        P(None, "ga", ("gx", "gy"), None),
        P("ga"),
        P("ga", ("gx", "gy"), None),
    )
    return jax.shard_map(
        local,
        mesh=mesh,
        in_specs=placed,
        out_specs=(P("ga", ("gx", "gy"), None), P("ga", ("gx", "gy"), None)),
        check_vma=False,
    )
```

```python
import functools
import math
import jax
import jax.numpy as jnp
from jax import lax
from jax.experimental import pallas as pl
from jax.experimental.pallas import tpu as pltpu
from jax.sharding import PartitionSpec as P

ENTRY = ((0, 3, 4), (3, 1, 5), (4, 5, 2))


def with_halo(block, sides, width):
    for axis, dim in sides:
        count = lax.axis_size(axis)
        forward = [(i, i + 1) for i in range(count - 1)]
        forward.append((count - 1, 0))
        backward = [(target, source) for source, target in forward]
        low = lax.ppermute(
            lax.slice_in_dim(block, block.shape[dim] - width, None, axis=dim), axis, forward
        )
        high = lax.ppermute(lax.slice_in_dim(block, 0, width, axis=dim), axis, backward)
        block = jnp.concatenate([low, block, high], axis=dim)
    return block


def central_last(field):
    return 0.5 * (jnp.roll(field, -1, 2) - jnp.roll(field, 1, 2))


def second_last(field):
    return jnp.roll(field, -1, 2) + jnp.roll(field, 1, 2) - 2.0 * field


def second_across(rimmed_block, member):
    return (
        rimmed_block[member, 1:-1, 2:]
        + rimmed_block[member, 1:-1, :-2]
        - 2.0 * rimmed_block[member, 1:-1, 1:-1]
    )


def hartley_matrix(points):
    counter = lax.iota(jnp.int32, points)
    product = counter[:, None] * counter[None, :] % points
    angles = 2.0 * jnp.pi / points * product.astype(jnp.float32)
    return (jnp.cos(angles) + jnp.sin(angles)) / jnp.sqrt(jnp.float32(points))


def solve_last(field, hartley_table, eigen):
    spectrum = (
        jnp.einsum("prn,nk->prk", field, hartley_table, precision=lax.Precision.HIGHEST)
        / eigen[:, None, :]
    )
    return jnp.einsum("prk,kn->prn", spectrum, hartley_table, precision=lax.Precision.HIGHEST)


def solve_swapped(field, hartley_table, eigen):
    spectrum = (
        jnp.einsum("prn,nk->prk", field, hartley_table, precision=lax.Precision.HIGHEST)
        / eigen[:, None, :]
    )
    return jnp.einsum("prk,kn->pnr", spectrum, hartley_table, precision=lax.Precision.HIGHEST)


def rimmed(stacked):
    return with_halo(stacked, ((("gx", "gy"), 2), ("ga", 1)), 1)


def gradients(rimmed_block, member, centre):
    grad_x = central_last(centre)
    grad_y = 0.5 * (rimmed_block[member, 1:-1, 2:] - rimmed_block[member, 1:-1, :-2])
    grad_z = 0.5 * (rimmed_block[member, 2:, 1:-1] - rimmed_block[member, :-2, 1:-1])
    return [grad_x, grad_y, grad_z]


def apply_tensor(tensor, rate_root, vectors):
    scales = (rate_root, rate_root, 1.0)
    results = []
    for target in range(3):
        total = jnp.zeros_like(vectors[0])
        for source in range(3):
            entry = tensor[ENTRY[target][source]].astype(jnp.float32)
            if target == source:
                entry = entry + 1.0
            total = total + scales[target] * scales[source] * entry * vectors[source]
        results.append(total)
    return results


def divergence(fluxes):
    rim_flux = with_halo(jnp.stack([fluxes[1], fluxes[2]]), ((("gx", "gy"), 2), ("ga", 1)), 1)
    across = 0.5 * (rim_flux[0, 1:-1, 2:] - rim_flux[0, 1:-1, :-2])
    planar = 0.5 * (rim_flux[1, 2:, 1:-1] - rim_flux[1, :-2, 1:-1])
    return central_last(fluxes[0]) + across + planar


def to_lines(block):
    return lax.all_to_all(block, ("gx", "gy"), split_axis=1, concat_axis=2, tiled=True)


def local_general(density, tensor, grad_u, plane_rate, cotangent):
    points = density.shape[2]
    hartley_table = hartley_matrix(points)
    modes = lax.iota(jnp.int32, points).astype(jnp.float32)
    eigen = (
        1.0 + 2.0 * plane_rate[:, None] * (1.0 - jnp.cos(2.0 * jnp.pi / points * modes))[None, :]
    )
    weight = plane_rate[:, None, None]
    rate_root = jnp.sqrt(weight)
    drift = [grad_u[member].astype(jnp.float32) for member in range(3)]
    rim_one = rimmed(density[None])
    grads = gradients(rim_one, 0, density)
    pushed = [grads[source] + drift[source] * density for source in range(3)]
    change = divergence(apply_tensor(tensor, rate_root, pushed))
    first = solve_swapped(density + change - weight * second_last(density), hartley_table, eigen)
    across = jnp.swapaxes(second_across(rim_one, 0), 1, 2)
    moved = to_lines(first - weight * across)
    new_density = solve_last(moved, hartley_table, eigen)
    swept = solve_swapped(cotangent, hartley_table, eigen)
    returned = to_lines(swept)
    settled = solve_last(returned, hartley_table, eigen)
    rim_two = rimmed(jnp.stack([settled, returned]))
    grads_two = gradients(rim_two, 0, settled)
    pulled = [-term for term in apply_tensor(tensor, rate_root, grads_two)]
    back = -divergence(pulled)
    for target in range(3):
        back = back + drift[target] * pulled[target]
    adjoint_density = (
        settled + back - weight * second_last(settled) - weight * second_across(rim_two, 1)
    )
    return (new_density, adjoint_density)


CHUNK = 256
STRIP = 16
LIMIT = 60 * 1024 * 1024


def decay_matrix(theta, kappa):
    row = lax.broadcasted_iota(jnp.int32, (CHUNK, CHUNK), 0)
    column = lax.broadcasted_iota(jnp.int32, (CHUNK, CHUNK), 1)
    distance = jnp.abs(row - column).astype(jnp.float32)
    return kappa * jnp.exp(-theta * distance)


def solve_lanes(field, par, plane):
    theta, kappa, wrap = par[plane, 2], par[plane, 3], par[plane, 4]
    matrix = decay_matrix(theta, kappa)
    count = field.shape[1] // CHUNK
    parts = [
        jnp.dot(
            field[:, CHUNK * a : CHUNK * (a + 1)],
            matrix,
            precision=lax.Precision.HIGHEST,
            preferred_element_type=jnp.float32,
        )
        for a in range(count)
    ]
    place = lax.broadcasted_iota(jnp.int32, (1, CHUNK), 1).astype(jnp.float32)
    rising = jnp.exp(-theta * (place + 1.0))
    falling = jnp.exp(-theta * (CHUNK - place))
    step = par[plane, 5]
    firsts = [part[:, :1] for part in parts]
    lasts = [part[:, CHUNK - 1 :] for part in parts]
    results = []
    for a in range(count):
        left = lasts[(a - count) % count]
        right = firsts[(a + count) % count]
        for m in range(count - 1, 0, -1):
            left = lasts[(a - m) % count] + step * left
            right = firsts[(a + m) % count] + step * right
        results.append(parts[a] + (wrap * left) * rising + (wrap * right) * falling)
    return results


def pack_plane(results, out_ref, slot, members, rows):
    whole = jnp.concatenate(results, axis=1)
    group = out_ref.shape[3] // rows
    for j in range(group):

        @pl.when(slot == j)
        def _():
            for d in range(members):
                out_ref[d, 0, :, rows * j : rows * (j + 1)] = whole[:, rows * d : rows * (d + 1)]


def lines_kernel(members, par, in_ref, out_ref):
    plane = pl.program_id(0)
    rows = in_ref.shape[1]
    group = out_ref.shape[3] // rows
    results = solve_lanes(in_ref[0], par, plane)
    pack_plane(results, out_ref, lax.rem(plane, group), members, rows)


def received_kernel(keep, par, in_ref, *outs):
    members, _, rows, lanes = in_ref.shape
    group = lanes // rows
    block = in_ref[:, 0].reshape(members * rows, lanes)
    turned = block.T
    for j in range(group):
        plane = pl.program_id(0) * group + j
        lines = turned[rows * j : rows * (j + 1)]
        results = solve_lanes(lines, par, plane)
        for a, part in enumerate(results):
            outs[0][j, :, CHUNK * a : CHUNK * (a + 1)] = part
        if keep:
            outs[1][j] = lines


def stencil_kernel(adjoint, members, par, rho, rho_z, rho_y, tensor, grad, rim_z, rim_y, *rest):
    if adjoint:
        other, other_y, out_ref, cell, flux_y, flux_z, partial = rest
    else:
        out_ref, cell, flux_y, flux_z, partial = rest
    planes, rows, lanes = rho.shape
    k = pl.program_id(0)
    now = lax.rem(k, 3)
    ring = lax.rem(k, 2)

    @pl.when(k == 0)
    def _():
        flux_z[2] = rim_z[0]

    @pl.when(k == planes)
    def _():
        flux_z[now] = rim_z[1]

    @pl.when(k < planes)
    def _():
        root = par[k, 1]
        scales = (root, root, 1.0)
        cell[8 : 8 + rows] = rho[k]
        cell[7:8] = rho_y[k, 0:1]
        cell[8 + rows : 9 + rows] = rho_y[k, 1:2]
        flux_y[7:8] = rim_y[k, 0:1]
        flux_y[8 + rows : 9 + rows] = rim_y[k, 1:2]
        before = jnp.maximum(k - 1, 0)
        after = jnp.minimum(k + 1, planes - 1)
        for s in range(rows // STRIP):
            top = STRIP * s
            span = slice(top, top + STRIP)
            centre = cell[8 + top : 8 + top + STRIP]
            low = jnp.where(k == 0, rho_z[0, span], rho[before, span])
            high = jnp.where(k == planes - 1, rho_z[1, span], rho[after, span])
            vectors = [
                0.5 * (pltpu.roll(centre, lanes - 1, 1) - pltpu.roll(centre, 1, 1)),
                0.5 * (cell[9 + top : 9 + top + STRIP] - cell[7 + top : 7 + top + STRIP]),
                0.5 * (high - low),
            ]
            drift = [grad[m, 0, span].astype(jnp.float32) for m in range(3)]
            if not adjoint:
                vectors = [vectors[m] + drift[m] * centre for m in range(3)]
            scaled = [scales[m] * vectors[m] for m in range(3)]
            entry = [tensor[m, 0, span].astype(jnp.float32) for m in range(6)]
            fluxes = []
            for target in range(3):
                total = scaled[target]
                for source in range(3):
                    total = total + entry[ENTRY[target][source]] * scaled[source]
                fluxes.append(total if target == 2 else root * total)
            change = 0.5 * (pltpu.roll(fluxes[0], lanes - 1, 1) - pltpu.roll(fluxes[0], 1, 1))
            if adjoint:
                for m in range(3):
                    change = change - drift[m] * fluxes[m]
            flux_y[8 + top : 8 + top + STRIP] = fluxes[1]
            flux_z[now, span] = fluxes[2]
            partial[ring, span] = change
        for s in range(rows // STRIP):
            top = STRIP * s
            span = slice(top, top + STRIP)
            partial[ring, span] = partial[ring, span] + 0.5 * (
                flux_y[9 + top : 9 + top + STRIP] - flux_y[7 + top : 7 + top + STRIP]
            )

    @pl.when(k > 0)
    def _():
        q = k - 1
        rate = par[q, 0]
        field, field_y = (other, other_y) if adjoint else (rho, rho_y)
        change = partial[1 - ring] + 0.5 * (flux_z[now] - flux_z[lax.rem(k + 1, 3)])
        pick = (q, slice(None), slice(None))
        if adjoint:
            centre = other[0]
            edge = other_y[q]
        else:
            centre = rho[pick]
            edge = rho_y[q]
        index = lax.broadcasted_iota(jnp.int32, (rows, lanes), 0)
        above = jnp.where(index == 0, edge[0:1], pltpu.roll(centre, 1, 0))
        below = jnp.where(index == rows - 1, edge[1:2], pltpu.roll(centre, rows - 1, 0))
        level = centre - rate * (above + below - 2.0 * centre)
        if adjoint:
            out_ref[0] = level + change
        else:
            parts = solve_lanes(change, par, q)
            parts = [
                part + level[:, CHUNK * a : CHUNK * (a + 1)] for a, part in enumerate(parts)
            ]
            group = out_ref.shape[3] // rows
            pack_plane(parts, out_ref, lax.rem(q, group), members, rows)


def exchange(low_edge, high_edge, axis):
    count = lax.axis_size(axis)
    forward = [(i, (i + 1) % count) for i in range(count)]
    backward = [(target, source) for source, target in forward]
    return lax.ppermute(high_edge, axis, forward), lax.ppermute(low_edge, axis, backward)


def rim_flux(target, centre, differences, tensor, grad, root, adjoint):
    scales = (root, root, 1.0)
    total = 0.0
    for source in range(3):
        vector = 0.5 * differences[source]
        if not adjoint:
            vector = vector + grad[source].astype(jnp.float32) * centre
        entry = tensor[ENTRY[target][source]].astype(jnp.float32)
        if target == source:
            entry = entry + 1.0
        total = total + scales[target] * scales[source] * entry * vector
    return total


def ends(array, axis):
    size = array.shape[axis]
    return jnp.concatenate(
        [lax.slice_in_dim(array, 0, 1, axis=axis), lax.slice_in_dim(array, size - 1, size, axis=axis)],
        axis,
    )


def flux_rims(field, field_z, field_y, field_z_y, outer_y, coupling_y, drift_y, tensor, grad, root, adjoint):
    def across_lanes(part):
        return jnp.roll(part, -1, 2) - jnp.roll(part, 1, 2)

    plane = ends(field, 0)
    above = jnp.concatenate([field_y[:, :1], field[:, :-1]], 1)[:: field.shape[0] - 1]
    below = jnp.concatenate([field[:, 1:], field_y[:, 1:]], 1)[:: field.shape[0] - 1]
    before = jnp.concatenate([field_z[:1], field[-2:-1]], 0)
    after = jnp.concatenate([field[1:2], field_z[1:]], 0)
    flux_z = rim_flux(
        2,
        plane,
        (across_lanes(plane), below - above, after - before),
        ends(tensor, 1),
        ends(grad, 1),
        ends(root, 0),
        adjoint,
    )
    z_low, z_high = exchange(flux_z[:1], flux_z[1:], "ga")
    sides = []
    for side in range(2):
        row = field_y[:, side : side + 1]
        corner = field_z_y[:, side : side + 1]
        before = jnp.concatenate([corner[:1], row[:-1]], 0)
        after = jnp.concatenate([row[1:], corner[1:]], 0)
        if side == 0:
            along = field[:, :1] - outer_y[:, :1]
        else:
            along = outer_y[:, 1:] - field[:, -1:]
        total = 0.0
        for source, difference in enumerate((across_lanes(row), along, after - before)):
            vector = 0.5 * difference
            if not adjoint:
                vector = vector + drift_y[side][:, source : source + 1] * row
            total = total + coupling_y[side][:, source : source + 1] * vector
        sides.append(total)
    return jnp.concatenate([z_low, z_high], 0), jnp.concatenate(sides, 1)


def edge_terms(tensor, grad, root, row):
    scales = (root, root, 1.0)
    terms = []
    for source in range(3):
        entry = lax.slice_in_dim(tensor[ENTRY[1][source]], row, row + 1, axis=1)
        entry = entry.astype(jnp.float32)
        if source == 1:
            entry = entry + 1.0
        terms.append(root * scales[source] * entry)
    for source in range(3):
        terms.append(lax.slice_in_dim(grad[source], row, row + 1, axis=1).astype(jnp.float32))
    return terms


def whole_block(array):
    zeros = (0,) * array.ndim
    return pl.BlockSpec(array.shape, lambda k: zeros)


def stencil(
    adjoint, members, group, par, root, field, field_y, outer_y, coupling_y, drift_y, tensor, grad, extra=()
):
    planes, rows, lanes = field.shape
    taller = jnp.concatenate([ends(field, 0), ends(field_y, 0)], 1)
    low, high = exchange(taller[:1], taller[1:], "ga")
    field_z = jnp.concatenate([low[:, :rows], high[:, :rows]], 0)
    field_z_y = jnp.concatenate([low[:, rows:], high[:, rows:]], 0)
    rim_z, rim_y = flux_rims(
        field, field_z, field_y, field_z_y, outer_y, coupling_y, drift_y, tensor, grad, root, adjoint
    )
    stream = lambda k: (0, jnp.minimum(k, planes - 1), 0, 0)
    specs = [
        pl.BlockSpec(memory_space=pltpu.SMEM),
        whole_block(field),
        whole_block(field_z),
        whole_block(field_y),
        pl.BlockSpec((6, 1, rows, lanes), stream),
        pl.BlockSpec((3, 1, rows, lanes), stream),
        whole_block(rim_z),
        whole_block(rim_y),
    ]
    args = [par, field, field_z, field_y, tensor, grad, rim_z, rim_y]
    if adjoint:
        other, other_y = extra
        specs += [
            pl.BlockSpec((1, rows, lanes), lambda k: (jnp.maximum(k - 1, 0), 0, 0)),
            whole_block(other_y),
        ]
        args += [other, other_y]
        out_shape = jax.ShapeDtypeStruct(field.shape, jnp.float32)
        out_spec = pl.BlockSpec((1, rows, lanes), lambda k: (jnp.maximum(k - 1, 0), 0, 0))
    else:
        out_shape = jax.ShapeDtypeStruct((members, planes // group, rows, group * rows), jnp.float32)
        out_spec = pl.BlockSpec(
            (members, 1, rows, group * rows), lambda k: (0, jnp.maximum(k - 1, 0) // group, 0, 0)
        )
    return pl.pallas_call(
        functools.partial(stencil_kernel, adjoint, members),
        grid=(planes + 1,),
        out_shape=out_shape,
        in_specs=specs,
        out_specs=out_spec,
        scratch_shapes=[
            pltpu.VMEM((rows + 16, lanes), jnp.float32),
            pltpu.VMEM((rows + 16, lanes), jnp.float32),
            pltpu.VMEM((3, rows, lanes), jnp.float32),
            pltpu.VMEM((2, rows, lanes), jnp.float32),
        ],
        compiler_params=pltpu.CompilerParams(vmem_limit_bytes=LIMIT),
        cost_estimate=pl.CostEstimate(
            flops=80 * field.size, bytes_accessed=32 * field.size, transcendentals=0
        ),
    )(*args)


def lines_solved(members, group, par, field):
    planes, rows, lanes = field.shape
    return pl.pallas_call(
        functools.partial(lines_kernel, members),
        grid=(planes,),
        out_shape=jax.ShapeDtypeStruct(
            (members, planes // group, rows, group * rows), jnp.float32
        ),
        in_specs=[
            pl.BlockSpec(memory_space=pltpu.SMEM),
            pl.BlockSpec((1, rows, lanes), lambda k: (k, 0, 0)),
        ],
        out_specs=pl.BlockSpec((members, 1, rows, group * rows), lambda k: (0, k // group, 0, 0)),
        compiler_params=pltpu.CompilerParams(vmem_limit_bytes=LIMIT),
        cost_estimate=pl.CostEstimate(
            flops=3072 * field.size, bytes_accessed=8 * field.size, transcendentals=0
        ),
    )(par, field)


def received_solved(keep, par, block):
    members, groups, rows, packed = block.shape
    group = packed // rows
    shape = jax.ShapeDtypeStruct((groups * group, rows, members * rows), jnp.float32)
    spec = pl.BlockSpec((group, rows, members * rows), lambda k: (k, 0, 0))
    return pl.pallas_call(
        functools.partial(received_kernel, keep),
        grid=(groups,),
        out_shape=[shape, shape] if keep else [shape],
        in_specs=[
            pl.BlockSpec(memory_space=pltpu.SMEM),
            pl.BlockSpec((members, 1, rows, packed), lambda k: (0, k, 0, 0)),
        ],
        out_specs=[spec, spec] if keep else [spec],
        compiler_params=pltpu.CompilerParams(vmem_limit_bytes=LIMIT),
        cost_estimate=pl.CostEstimate(
            flops=3072 * block.size, bytes_accessed=8 * block.size, transcendentals=0
        ),
    )(par, block)


def traded(block):
    return lax.all_to_all(block, ("gx", "gy"), split_axis=0, concat_axis=0, tiled=True)


def local(density, tensor, grad_u, plane_rate, cotangent):
    planes, rows, lanes = density.shape
    members = lanes // rows
    group = 128 // math.gcd(rows, 128)
    if rows % STRIP or planes % group or lanes % CHUNK:
        return local_general(density, tensor, grad_u, plane_rate, cotangent)
    root = jnp.sqrt(plane_rate)
    half = 0.5 / root
    theta = 2.0 * jnp.log1p(half + half * half / (1.0 + jnp.sqrt(1.0 + half * half)))
    kappa = 1.0 / jnp.sqrt(1.0 + 4.0 * plane_rate)
    wrap = 1.0 / (1.0 - jnp.exp(-theta * lanes))
    step = jnp.exp(-theta * CHUNK)
    par = jnp.stack([plane_rate, root, theta, kappa, wrap, step], 1)
    root = root[:, None, None]
    low, high = exchange(
        jnp.concatenate([density[:, :2]] + edge_terms(tensor, grad_u, root, 0), 1),
        jnp.concatenate([density[:, -2:]] + edge_terms(tensor, grad_u, root, rows - 1), 1),
        ("gx", "gy"),
    )
    swept = lines_solved(members, group, par, cotangent)
    swept, low, high = lax.optimization_barrier((swept, low, high))
    swept = traded(swept)
    coupling_y = (low[:, 2:5], high[:, 2:5])
    drift_y = (low[:, 5:8], high[:, 5:8])
    packed = stencil(
        False,
        members,
        group,
        par,
        root,
        density,
        jnp.concatenate([low[:, 1:2], high[:, :1]], 1),
        jnp.concatenate([low[:, :1], high[:, 1:2]], 1),
        coupling_y,
        drift_y,
        tensor,
        grad_u,
    )
    packed, swept = lax.optimization_barrier((packed, swept))
    settled, returned = received_solved(True, par, swept)
    low, high = exchange(
        jnp.concatenate([settled[:, :2], returned[:, :1]], 1),
        jnp.concatenate([settled[:, -2:], returned[:, -1:]], 1),
        ("gx", "gy"),
    )
    packed, low, high = lax.optimization_barrier((packed, low, high))
    moved = traded(packed)
    adjoint_density = stencil(
        True,
        members,
        group,
        par,
        root,
        settled,
        jnp.concatenate([low[:, 1:2], high[:, :1]], 1),
        jnp.concatenate([low[:, :1], high[:, 1:2]], 1),
        coupling_y,
        drift_y,
        tensor,
        grad_u,
        (returned, jnp.concatenate([low[:, 2:], high[:, 2:]], 1)),
    )
    moved, adjoint_density = lax.optimization_barrier((moved, adjoint_density))
    (new_density,) = received_solved(False, par, moved)
    return (new_density, adjoint_density)


def solution(mesh):
    placed = (
        P("ga", ("gx", "gy"), None),
        P(None, "ga", ("gx", "gy"), None),
        P(None, "ga", ("gx", "gy"), None),
        P("ga"),
        P("ga", ("gx", "gy"), None),
    )
    return jax.shard_map(
        local,
        mesh=mesh,
        in_specs=placed,
        out_specs=(P("ga", ("gx", "gy"), None), P("ga", ("gx", "gy"), None)),
        check_vma=False,
    )
```

```python
import functools
import math
import jax
import jax.numpy as jnp
from jax import lax
from jax.experimental import pallas as pl
from jax.experimental.pallas import tpu as pltpu
from jax.sharding import PartitionSpec as P

ENTRY = ((0, 3, 4), (3, 1, 5), (4, 5, 2))


def with_halo(block, sides, width):
    for axis, dim in sides:
        count = lax.axis_size(axis)
        forward = [(i, i + 1) for i in range(count - 1)]
        forward.append((count - 1, 0))
        backward = [(target, source) for source, target in forward]
        low = lax.ppermute(
            lax.slice_in_dim(block, block.shape[dim] - width, None, axis=dim), axis, forward
        )
        high = lax.ppermute(lax.slice_in_dim(block, 0, width, axis=dim), axis, backward)
        block = jnp.concatenate([low, block, high], axis=dim)
    return block


def central_last(field):
    return 0.5 * (jnp.roll(field, -1, 2) - jnp.roll(field, 1, 2))


def second_last(field):
    return jnp.roll(field, -1, 2) + jnp.roll(field, 1, 2) - 2.0 * field


def second_across(rimmed_block, member):
    return (
        rimmed_block[member, 1:-1, 2:]
        + rimmed_block[member, 1:-1, :-2]
        - 2.0 * rimmed_block[member, 1:-1, 1:-1]
    )


def hartley_matrix(points):
    counter = lax.iota(jnp.int32, points)
    product = counter[:, None] * counter[None, :] % points
    angles = 2.0 * jnp.pi / points * product.astype(jnp.float32)
    return (jnp.cos(angles) + jnp.sin(angles)) / jnp.sqrt(jnp.float32(points))


def solve_last(field, hartley_table, eigen):
    spectrum = (
        jnp.einsum("prn,nk->prk", field, hartley_table, precision=lax.Precision.HIGHEST)
        / eigen[:, None, :]
    )
    return jnp.einsum("prk,kn->prn", spectrum, hartley_table, precision=lax.Precision.HIGHEST)


def solve_swapped(field, hartley_table, eigen):
    spectrum = (
        jnp.einsum("prn,nk->prk", field, hartley_table, precision=lax.Precision.HIGHEST)
        / eigen[:, None, :]
    )
    return jnp.einsum("prk,kn->pnr", spectrum, hartley_table, precision=lax.Precision.HIGHEST)


def rimmed(stacked):
    return with_halo(stacked, ((("gx", "gy"), 2), ("ga", 1)), 1)


def gradients(rimmed_block, member, centre):
    grad_x = central_last(centre)
    grad_y = 0.5 * (rimmed_block[member, 1:-1, 2:] - rimmed_block[member, 1:-1, :-2])
    grad_z = 0.5 * (rimmed_block[member, 2:, 1:-1] - rimmed_block[member, :-2, 1:-1])
    return [grad_x, grad_y, grad_z]


def apply_tensor(tensor, rate_root, vectors):
    scales = (rate_root, rate_root, 1.0)
    results = []
    for target in range(3):
        total = jnp.zeros_like(vectors[0])
        for source in range(3):
            entry = tensor[ENTRY[target][source]].astype(jnp.float32)
            if target == source:
                entry = entry + 1.0
            total = total + scales[target] * scales[source] * entry * vectors[source]
        results.append(total)
    return results


def divergence(fluxes):
    rim_flux = with_halo(jnp.stack([fluxes[1], fluxes[2]]), ((("gx", "gy"), 2), ("ga", 1)), 1)
    across = 0.5 * (rim_flux[0, 1:-1, 2:] - rim_flux[0, 1:-1, :-2])
    planar = 0.5 * (rim_flux[1, 2:, 1:-1] - rim_flux[1, :-2, 1:-1])
    return central_last(fluxes[0]) + across + planar


def to_lines(block):
    return lax.all_to_all(block, ("gx", "gy"), split_axis=1, concat_axis=2, tiled=True)


def local_general(density, tensor, grad_u, plane_rate, cotangent):
    points = density.shape[2]
    hartley_table = hartley_matrix(points)
    modes = lax.iota(jnp.int32, points).astype(jnp.float32)
    eigen = (
        1.0 + 2.0 * plane_rate[:, None] * (1.0 - jnp.cos(2.0 * jnp.pi / points * modes))[None, :]
    )
    weight = plane_rate[:, None, None]
    rate_root = jnp.sqrt(weight)
    drift = [grad_u[member].astype(jnp.float32) for member in range(3)]
    rim_one = rimmed(density[None])
    grads = gradients(rim_one, 0, density)
    pushed = [grads[source] + drift[source] * density for source in range(3)]
    change = divergence(apply_tensor(tensor, rate_root, pushed))
    first = solve_swapped(density + change - weight * second_last(density), hartley_table, eigen)
    across = jnp.swapaxes(second_across(rim_one, 0), 1, 2)
    moved = to_lines(first - weight * across)
    new_density = solve_last(moved, hartley_table, eigen)
    swept = solve_swapped(cotangent, hartley_table, eigen)
    returned = to_lines(swept)
    settled = solve_last(returned, hartley_table, eigen)
    rim_two = rimmed(jnp.stack([settled, returned]))
    grads_two = gradients(rim_two, 0, settled)
    pulled = [-term for term in apply_tensor(tensor, rate_root, grads_two)]
    back = -divergence(pulled)
    for target in range(3):
        back = back + drift[target] * pulled[target]
    adjoint_density = (
        settled + back - weight * second_last(settled) - weight * second_across(rim_two, 1)
    )
    return (new_density, adjoint_density)


CHUNK = 256
STRIP = 16
LIMIT = 60 * 1024 * 1024


def decay_matrix(theta, kappa):
    row = lax.broadcasted_iota(jnp.int32, (CHUNK, CHUNK), 0)
    column = lax.broadcasted_iota(jnp.int32, (CHUNK, CHUNK), 1)
    distance = jnp.abs(row - column).astype(jnp.float32)
    return kappa * jnp.exp(-theta * distance)


def solve_lanes(field, par, plane):
    theta, kappa, wrap = par[plane, 2], par[plane, 3], par[plane, 4]
    matrix = decay_matrix(theta, kappa)
    count = field.shape[1] // CHUNK
    parts = [
        jnp.dot(
            field[:, CHUNK * a : CHUNK * (a + 1)],
            matrix,
            precision=lax.Precision.HIGHEST,
            preferred_element_type=jnp.float32,
        )
        for a in range(count)
    ]
    place = lax.broadcasted_iota(jnp.int32, (1, CHUNK), 1).astype(jnp.float32)
    rising = jnp.exp(-theta * (place + 1.0))
    falling = jnp.exp(-theta * (CHUNK - place))
    step = par[plane, 5]
    firsts = [part[:, :1] for part in parts]
    lasts = [part[:, CHUNK - 1 :] for part in parts]
    results = []
    for a in range(count):
        left = lasts[(a - count) % count]
        right = firsts[(a + count) % count]
        for m in range(count - 1, 0, -1):
            left = lasts[(a - m) % count] + step * left
            right = firsts[(a + m) % count] + step * right
        results.append(parts[a] + (wrap * left) * rising + (wrap * right) * falling)
    return results


def pack_plane(results, out_ref, slot, members, rows):
    whole = jnp.concatenate(results, axis=1)
    group = out_ref.shape[3] // rows
    for j in range(group):

        @pl.when(slot == j)
        def _():
            for d in range(members):
                out_ref[d, 0, :, rows * j : rows * (j + 1)] = whole[:, rows * d : rows * (d + 1)]


def lines_kernel(members, par, in_ref, out_ref):
    group, rows, _ = in_ref.shape
    for j in range(group):
        results = solve_lanes(in_ref[j], par, pl.program_id(0) * group + j)
        whole = jnp.concatenate(results, axis=1)
        for d in range(members):
            out_ref[d, 0, :, rows * j : rows * (j + 1)] = whole[:, rows * d : rows * (d + 1)]


def received_kernel(keep, par, in_ref, *outs):
    members, _, rows, lanes = in_ref.shape
    group = lanes // rows
    block = in_ref[:, 0].reshape(members * rows, lanes)
    turned = block.T
    for j in range(group):
        plane = pl.program_id(0) * group + j
        lines = turned[rows * j : rows * (j + 1)]
        results = solve_lanes(lines, par, plane)
        for a, part in enumerate(results):
            outs[0][j, :, CHUNK * a : CHUNK * (a + 1)] = part
        if keep:
            outs[1][j] = lines


def stencil_kernel(adjoint, members, par, rho, rho_z, rho_y, tensor, grad, rim_z, rim_y, *rest):
    if adjoint:
        other, other_y, out_ref, cell, flux_y, flux_z, partial = rest
    else:
        out_ref, cell, flux_y, flux_z, partial = rest
    planes, rows, lanes = rho.shape
    k = pl.program_id(0)
    now = lax.rem(k, 3)
    ring = lax.rem(k, 2)

    @pl.when(k == 0)
    def _():
        flux_z[2] = rim_z[0]

    @pl.when(k == planes)
    def _():
        flux_z[now] = rim_z[1]

    @pl.when(k < planes)
    def _():
        root = par[k, 1]
        scales = (root, root, 1.0)
        cell[8 : 8 + rows] = rho[k]
        cell[7:8] = rho_y[k, 0:1]
        cell[8 + rows : 9 + rows] = rho_y[k, 1:2]
        flux_y[7:8] = rim_y[k, 0:1]
        flux_y[8 + rows : 9 + rows] = rim_y[k, 1:2]
        before = jnp.maximum(k - 1, 0)
        after = jnp.minimum(k + 1, planes - 1)
        for s in range(rows // STRIP):
            top = STRIP * s
            span = slice(top, top + STRIP)
            centre = cell[8 + top : 8 + top + STRIP]
            low = jnp.where(k == 0, rho_z[0, span], rho[before, span])
            high = jnp.where(k == planes - 1, rho_z[1, span], rho[after, span])
            vectors = [
                0.5 * (pltpu.roll(centre, lanes - 1, 1) - pltpu.roll(centre, 1, 1)),
                0.5 * (cell[9 + top : 9 + top + STRIP] - cell[7 + top : 7 + top + STRIP]),
                0.5 * (high - low),
            ]
            drift = [grad[m, 0, span].astype(jnp.float32) for m in range(3)]
            if not adjoint:
                vectors = [vectors[m] + drift[m] * centre for m in range(3)]
            scaled = [scales[m] * vectors[m] for m in range(3)]
            entry = [tensor[m, 0, span].astype(jnp.float32) for m in range(6)]
            fluxes = []
            for target in range(3):
                total = scaled[target]
                for source in range(3):
                    total = total + entry[ENTRY[target][source]] * scaled[source]
                fluxes.append(total if target == 2 else root * total)
            change = 0.5 * (pltpu.roll(fluxes[0], lanes - 1, 1) - pltpu.roll(fluxes[0], 1, 1))
            if adjoint:
                for m in range(3):
                    change = change - drift[m] * fluxes[m]
            flux_y[8 + top : 8 + top + STRIP] = fluxes[1]
            flux_z[now, span] = fluxes[2]
            partial[ring, span] = change
        for s in range(rows // STRIP):
            top = STRIP * s
            span = slice(top, top + STRIP)
            partial[ring, span] = partial[ring, span] + 0.5 * (
                flux_y[9 + top : 9 + top + STRIP] - flux_y[7 + top : 7 + top + STRIP]
            )

    @pl.when(k > 0)
    def _():
        q = k - 1
        rate = par[q, 0]
        field, field_y = (other, other_y) if adjoint else (rho, rho_y)
        change = partial[1 - ring] + 0.5 * (flux_z[now] - flux_z[lax.rem(k + 1, 3)])
        pick = (q, slice(None), slice(None))
        if adjoint:
            centre = other[0]
            edge = other_y[q]
        else:
            centre = rho[pick]
            edge = rho_y[q]
        index = lax.broadcasted_iota(jnp.int32, (rows, lanes), 0)
        above = jnp.where(index == 0, edge[0:1], pltpu.roll(centre, 1, 0))
        below = jnp.where(index == rows - 1, edge[1:2], pltpu.roll(centre, rows - 1, 0))
        level = centre - rate * (above + below - 2.0 * centre)
        if adjoint:
            out_ref[0] = level + change
        else:
            parts = solve_lanes(change, par, q)
            parts = [
                part + level[:, CHUNK * a : CHUNK * (a + 1)] for a, part in enumerate(parts)
            ]
            group = out_ref.shape[3] // rows
            pack_plane(parts, out_ref, lax.rem(q, group), members, rows)


def exchange(low_edge, high_edge, axis):
    count = lax.axis_size(axis)
    forward = [(i, (i + 1) % count) for i in range(count)]
    backward = [(target, source) for source, target in forward]
    return lax.ppermute(high_edge, axis, forward), lax.ppermute(low_edge, axis, backward)


def rim_flux(target, centre, differences, tensor, grad, root, adjoint):
    scales = (root, root, 1.0)
    total = 0.0
    for source in range(3):
        vector = 0.5 * differences[source]
        if not adjoint:
            vector = vector + grad[source].astype(jnp.float32) * centre
        entry = tensor[ENTRY[target][source]].astype(jnp.float32)
        if target == source:
            entry = entry + 1.0
        total = total + scales[target] * scales[source] * entry * vector
    return total


def ends(array, axis):
    size = array.shape[axis]
    return jnp.concatenate(
        [lax.slice_in_dim(array, 0, 1, axis=axis), lax.slice_in_dim(array, size - 1, size, axis=axis)],
        axis,
    )


def flux_rims(field, field_z, field_y, field_z_y, outer_y, coupling_y, drift_y, tensor, grad, root, adjoint):
    def across_lanes(part):
        return jnp.roll(part, -1, 2) - jnp.roll(part, 1, 2)

    plane = ends(field, 0)
    outer = ends(field_y, 0)
    above = jnp.concatenate([outer[:, :1], plane[:, :-1]], 1)
    below = jnp.concatenate([plane[:, 1:], outer[:, 1:]], 1)
    before = jnp.concatenate([field_z[:1], field[-2:-1]], 0)
    after = jnp.concatenate([field[1:2], field_z[1:]], 0)
    flux_z = rim_flux(
        2,
        plane,
        (across_lanes(plane), below - above, after - before),
        ends(tensor, 1),
        ends(grad, 1),
        ends(root, 0),
        adjoint,
    )
    z_low, z_high = exchange(flux_z[:1], flux_z[1:], "ga")
    sides = []
    for side in range(2):
        row = field_y[:, side : side + 1]
        corner = field_z_y[:, side : side + 1]
        before = jnp.concatenate([corner[:1], row[:-1]], 0)
        after = jnp.concatenate([row[1:], corner[1:]], 0)
        if side == 0:
            along = field[:, :1] - outer_y[:, :1]
        else:
            along = outer_y[:, 1:] - field[:, -1:]
        total = 0.0
        for source, difference in enumerate((across_lanes(row), along, after - before)):
            vector = 0.5 * difference
            if not adjoint:
                vector = vector + drift_y[side][:, source : source + 1] * row
            total = total + coupling_y[side][:, source : source + 1] * vector
        sides.append(total)
    return jnp.concatenate([z_low, z_high], 0), jnp.concatenate(sides, 1)


def edge_row(array, member, row):
    planes, lanes = array.shape[1], array.shape[3]
    part = lax.slice(array, (member, 0, row, 0), (member + 1, planes, row + 1, lanes))
    return part.reshape(planes, 1, lanes).astype(jnp.float32)


def edge_terms(tensor, grad, root, row):
    scales = (root, root, 1.0)
    terms = []
    for source in range(3):
        entry = edge_row(tensor, ENTRY[1][source], row)
        if source == 1:
            entry = entry + 1.0
        terms.append(root * scales[source] * entry)
    for source in range(3):
        terms.append(edge_row(grad, source, row))
    return terms


def whole_block(array):
    zeros = (0,) * array.ndim
    return pl.BlockSpec(array.shape, lambda k: zeros)


def stencil(
    adjoint, members, group, par, root, field, field_y, outer_y, coupling_y, drift_y, tensor, grad, extra=()
):
    planes, rows, lanes = field.shape
    taller = jnp.concatenate([ends(field, 0), ends(field_y, 0)], 1)
    low, high = exchange(taller[:1], taller[1:], "ga")
    field_z = jnp.concatenate([low[:, :rows], high[:, :rows]], 0)
    field_z_y = jnp.concatenate([low[:, rows:], high[:, rows:]], 0)
    rim_z, rim_y = flux_rims(
        field, field_z, field_y, field_z_y, outer_y, coupling_y, drift_y, tensor, grad, root, adjoint
    )
    stream = lambda k: (0, jnp.minimum(k, planes - 1), 0, 0)
    specs = [
        pl.BlockSpec(memory_space=pltpu.SMEM),
        whole_block(field),
        whole_block(field_z),
        whole_block(field_y),
        pl.BlockSpec((6, 1, rows, lanes), stream),
        pl.BlockSpec((3, 1, rows, lanes), stream),
        whole_block(rim_z),
        whole_block(rim_y),
    ]
    args = [par, field, field_z, field_y, tensor, grad, rim_z, rim_y]
    if adjoint:
        other, other_y = extra
        specs += [
            pl.BlockSpec((1, rows, lanes), lambda k: (jnp.maximum(k - 1, 0), 0, 0)),
            whole_block(other_y),
        ]
        args += [other, other_y]
        out_shape = jax.ShapeDtypeStruct(field.shape, jnp.float32)
        out_spec = pl.BlockSpec((1, rows, lanes), lambda k: (jnp.maximum(k - 1, 0), 0, 0))
    else:
        out_shape = jax.ShapeDtypeStruct((members, planes // group, rows, group * rows), jnp.float32)
        out_spec = pl.BlockSpec(
            (members, 1, rows, group * rows), lambda k: (0, jnp.maximum(k - 1, 0) // group, 0, 0)
        )
    return pl.pallas_call(
        functools.partial(stencil_kernel, adjoint, members),
        grid=(planes + 1,),
        out_shape=out_shape,
        in_specs=specs,
        out_specs=out_spec,
        scratch_shapes=[
            pltpu.VMEM((rows + 16, lanes), jnp.float32),
            pltpu.VMEM((rows + 16, lanes), jnp.float32),
            pltpu.VMEM((3, rows, lanes), jnp.float32),
            pltpu.VMEM((2, rows, lanes), jnp.float32),
        ],
        compiler_params=pltpu.CompilerParams(vmem_limit_bytes=LIMIT),
        cost_estimate=pl.CostEstimate(
            flops=80 * field.size, bytes_accessed=32 * field.size, transcendentals=0
        ),
    )(*args)


def lines_solved(members, group, par, field):
    planes, rows, lanes = field.shape
    return pl.pallas_call(
        functools.partial(lines_kernel, members),
        grid=(planes // group,),
        out_shape=jax.ShapeDtypeStruct(
            (members, planes // group, rows, group * rows), jnp.float32
        ),
        in_specs=[
            pl.BlockSpec(memory_space=pltpu.SMEM),
            pl.BlockSpec((group, rows, lanes), lambda k: (k, 0, 0)),
        ],
        out_specs=pl.BlockSpec((members, 1, rows, group * rows), lambda k: (0, k, 0, 0)),
        compiler_params=pltpu.CompilerParams(vmem_limit_bytes=LIMIT),
        cost_estimate=pl.CostEstimate(
            flops=3072 * field.size, bytes_accessed=8 * field.size, transcendentals=0
        ),
    )(par, field)


def received_solved(keep, par, block):
    members, groups, rows, packed = block.shape
    group = packed // rows
    shape = jax.ShapeDtypeStruct((groups * group, rows, members * rows), jnp.float32)
    spec = pl.BlockSpec((group, rows, members * rows), lambda k: (k, 0, 0))
    return pl.pallas_call(
        functools.partial(received_kernel, keep),
        grid=(groups,),
        out_shape=[shape, shape] if keep else [shape],
        in_specs=[
            pl.BlockSpec(memory_space=pltpu.SMEM),
            pl.BlockSpec((members, 1, rows, packed), lambda k: (0, k, 0, 0)),
        ],
        out_specs=[spec, spec] if keep else [spec],
        compiler_params=pltpu.CompilerParams(vmem_limit_bytes=LIMIT),
        cost_estimate=pl.CostEstimate(
            flops=3072 * block.size, bytes_accessed=8 * block.size, transcendentals=0
        ),
    )(par, block)


def traded(block):
    return lax.all_to_all(block, ("gx", "gy"), split_axis=0, concat_axis=0, tiled=True)


def local(density, tensor, grad_u, plane_rate, cotangent):
    planes, rows, lanes = density.shape
    members = lanes // rows
    group = 128 // math.gcd(rows, 128)
    if rows % STRIP or planes % group or lanes % CHUNK:
        return local_general(density, tensor, grad_u, plane_rate, cotangent)
    root = jnp.sqrt(plane_rate)
    half = 0.5 / root
    theta = 2.0 * jnp.log1p(half + half * half / (1.0 + jnp.sqrt(1.0 + half * half)))
    kappa = 1.0 / jnp.sqrt(1.0 + 4.0 * plane_rate)
    wrap = 1.0 / (1.0 - jnp.exp(-theta * lanes))
    step = jnp.exp(-theta * CHUNK)
    par = jnp.stack([plane_rate, root, theta, kappa, wrap, step], 1)
    root = root[:, None, None]
    low, high = exchange(
        jnp.concatenate([density[:, :2]] + edge_terms(tensor, grad_u, root, 0), 1),
        jnp.concatenate([density[:, -2:]] + edge_terms(tensor, grad_u, root, rows - 1), 1),
        ("gx", "gy"),
    )
    swept = lines_solved(members, group, par, cotangent)
    swept, low, high = lax.optimization_barrier((swept, low, high))
    swept = traded(swept)
    coupling_y = (low[:, 2:5], high[:, 2:5])
    drift_y = (low[:, 5:8], high[:, 5:8])
    packed = stencil(
        False,
        members,
        group,
        par,
        root,
        density,
        jnp.concatenate([low[:, 1:2], high[:, :1]], 1),
        jnp.concatenate([low[:, :1], high[:, 1:2]], 1),
        coupling_y,
        drift_y,
        tensor,
        grad_u,
    )
    packed, swept = lax.optimization_barrier((packed, swept))
    settled, returned = received_solved(True, par, swept)
    low, high = exchange(
        jnp.concatenate([settled[:, :2], returned[:, :1]], 1),
        jnp.concatenate([settled[:, -2:], returned[:, -1:]], 1),
        ("gx", "gy"),
    )
    packed, low, high = lax.optimization_barrier((packed, low, high))
    moved = traded(packed)
    adjoint_density = stencil(
        True,
        members,
        group,
        par,
        root,
        settled,
        jnp.concatenate([low[:, 1:2], high[:, :1]], 1),
        jnp.concatenate([low[:, :1], high[:, 1:2]], 1),
        coupling_y,
        drift_y,
        tensor,
        grad_u,
        (returned, jnp.concatenate([low[:, 2:], high[:, 2:]], 1)),
    )
    moved, adjoint_density = lax.optimization_barrier((moved, adjoint_density))
    (new_density,) = received_solved(False, par, moved)
    return (new_density, adjoint_density)


def solution(mesh):
    placed = (
        P("ga", ("gx", "gy"), None),
        P(None, "ga", ("gx", "gy"), None),
        P(None, "ga", ("gx", "gy"), None),
        P("ga"),
        P("ga", ("gx", "gy"), None),
    )
    return jax.shard_map(
        local,
        mesh=mesh,
        in_specs=placed,
        out_specs=(P("ga", ("gx", "gy"), None), P("ga", ("gx", "gy"), None)),
        check_vma=False,
    )
```

```python
import functools
import math
import jax
import jax.numpy as jnp
from jax import lax
from jax.experimental import pallas as pl
from jax.experimental.pallas import tpu as pltpu
from jax.sharding import PartitionSpec as P

ENTRY = ((0, 3, 4), (3, 1, 5), (4, 5, 2))


def with_halo(block, sides, width):
    for axis, dim in sides:
        count = lax.axis_size(axis)
        forward = [(i, i + 1) for i in range(count - 1)]
        forward.append((count - 1, 0))
        backward = [(target, source) for source, target in forward]
        low = lax.ppermute(
            lax.slice_in_dim(block, block.shape[dim] - width, None, axis=dim), axis, forward
        )
        high = lax.ppermute(lax.slice_in_dim(block, 0, width, axis=dim), axis, backward)
        block = jnp.concatenate([low, block, high], axis=dim)
    return block


def central_last(field):
    return 0.5 * (jnp.roll(field, -1, 2) - jnp.roll(field, 1, 2))


def second_last(field):
    return jnp.roll(field, -1, 2) + jnp.roll(field, 1, 2) - 2.0 * field


def second_across(rimmed_block, member):
    return (
        rimmed_block[member, 1:-1, 2:]
        + rimmed_block[member, 1:-1, :-2]
        - 2.0 * rimmed_block[member, 1:-1, 1:-1]
    )


def hartley_matrix(points):
    counter = lax.iota(jnp.int32, points)
    product = counter[:, None] * counter[None, :] % points
    angles = 2.0 * jnp.pi / points * product.astype(jnp.float32)
    return (jnp.cos(angles) + jnp.sin(angles)) / jnp.sqrt(jnp.float32(points))


def solve_last(field, hartley_table, eigen):
    spectrum = (
        jnp.einsum("prn,nk->prk", field, hartley_table, precision=lax.Precision.HIGHEST)
        / eigen[:, None, :]
    )
    return jnp.einsum("prk,kn->prn", spectrum, hartley_table, precision=lax.Precision.HIGHEST)


def solve_swapped(field, hartley_table, eigen):
    spectrum = (
        jnp.einsum("prn,nk->prk", field, hartley_table, precision=lax.Precision.HIGHEST)
        / eigen[:, None, :]
    )
    return jnp.einsum("prk,kn->pnr", spectrum, hartley_table, precision=lax.Precision.HIGHEST)


def rimmed(stacked):
    return with_halo(stacked, ((("gx", "gy"), 2), ("ga", 1)), 1)


def gradients(rimmed_block, member, centre):
    grad_x = central_last(centre)
    grad_y = 0.5 * (rimmed_block[member, 1:-1, 2:] - rimmed_block[member, 1:-1, :-2])
    grad_z = 0.5 * (rimmed_block[member, 2:, 1:-1] - rimmed_block[member, :-2, 1:-1])
    return [grad_x, grad_y, grad_z]


def apply_tensor(tensor, rate_root, vectors):
    scales = (rate_root, rate_root, 1.0)
    results = []
    for target in range(3):
        total = jnp.zeros_like(vectors[0])
        for source in range(3):
            entry = tensor[ENTRY[target][source]].astype(jnp.float32)
            if target == source:
                entry = entry + 1.0
            total = total + scales[target] * scales[source] * entry * vectors[source]
        results.append(total)
    return results


def divergence(fluxes):
    rim_flux = with_halo(jnp.stack([fluxes[1], fluxes[2]]), ((("gx", "gy"), 2), ("ga", 1)), 1)
    across = 0.5 * (rim_flux[0, 1:-1, 2:] - rim_flux[0, 1:-1, :-2])
    planar = 0.5 * (rim_flux[1, 2:, 1:-1] - rim_flux[1, :-2, 1:-1])
    return central_last(fluxes[0]) + across + planar


def to_lines(block):
    return lax.all_to_all(block, ("gx", "gy"), split_axis=1, concat_axis=2, tiled=True)


def local_general(density, tensor, grad_u, plane_rate, cotangent):
    points = density.shape[2]
    hartley_table = hartley_matrix(points)
    modes = lax.iota(jnp.int32, points).astype(jnp.float32)
    eigen = (
        1.0 + 2.0 * plane_rate[:, None] * (1.0 - jnp.cos(2.0 * jnp.pi / points * modes))[None, :]
    )
    weight = plane_rate[:, None, None]
    rate_root = jnp.sqrt(weight)
    drift = [grad_u[member].astype(jnp.float32) for member in range(3)]
    rim_one = rimmed(density[None])
    grads = gradients(rim_one, 0, density)
    pushed = [grads[source] + drift[source] * density for source in range(3)]
    change = divergence(apply_tensor(tensor, rate_root, pushed))
    first = solve_swapped(density + change - weight * second_last(density), hartley_table, eigen)
    across = jnp.swapaxes(second_across(rim_one, 0), 1, 2)
    moved = to_lines(first - weight * across)
    new_density = solve_last(moved, hartley_table, eigen)
    swept = solve_swapped(cotangent, hartley_table, eigen)
    returned = to_lines(swept)
    settled = solve_last(returned, hartley_table, eigen)
    rim_two = rimmed(jnp.stack([settled, returned]))
    grads_two = gradients(rim_two, 0, settled)
    pulled = [-term for term in apply_tensor(tensor, rate_root, grads_two)]
    back = -divergence(pulled)
    for target in range(3):
        back = back + drift[target] * pulled[target]
    adjoint_density = (
        settled + back - weight * second_last(settled) - weight * second_across(rim_two, 1)
    )
    return (new_density, adjoint_density)


CHUNK = 256
STRIP = 16
LIMIT = 60 * 1024 * 1024


def decay_matrix(theta, kappa):
    row = lax.broadcasted_iota(jnp.int32, (CHUNK, CHUNK), 0)
    column = lax.broadcasted_iota(jnp.int32, (CHUNK, CHUNK), 1)
    distance = jnp.abs(row - column).astype(jnp.float32)
    return kappa * jnp.exp(-theta * distance)


def solve_lanes(field, par, plane):
    theta, kappa, wrap = par[plane, 2], par[plane, 3], par[plane, 4]
    matrix = decay_matrix(theta, kappa)
    count = field.shape[1] // CHUNK
    parts = [
        jnp.dot(
            field[:, CHUNK * a : CHUNK * (a + 1)],
            matrix,
            precision=lax.Precision.HIGHEST,
            preferred_element_type=jnp.float32,
        )
        for a in range(count)
    ]
    place = lax.broadcasted_iota(jnp.int32, (1, CHUNK), 1).astype(jnp.float32)
    rising = jnp.exp(-theta * (place + 1.0))
    falling = jnp.exp(-theta * (CHUNK - place))
    step = par[plane, 5]
    firsts = [part[:, :1] for part in parts]
    lasts = [part[:, CHUNK - 1 :] for part in parts]
    results = []
    for a in range(count):
        left = lasts[(a - count) % count]
        right = firsts[(a + count) % count]
        for m in range(count - 1, 0, -1):
            left = lasts[(a - m) % count] + step * left
            right = firsts[(a + m) % count] + step * right
        results.append(parts[a] + (wrap * left) * rising + (wrap * right) * falling)
    return results


def pack_plane(results, out_ref, slot, members, rows):
    whole = jnp.concatenate(results, axis=1)
    group = out_ref.shape[3] // rows
    for j in range(group):

        @pl.when(slot == j)
        def _():
            for d in range(members):
                out_ref[d, 0, :, rows * j : rows * (j + 1)] = whole[:, rows * d : rows * (d + 1)]


def lines_kernel(members, par, in_ref, out_ref):
    group, rows, _ = in_ref.shape
    for j in range(group):
        results = solve_lanes(in_ref[j], par, pl.program_id(0) * group + j)
        whole = jnp.concatenate(results, axis=1)
        for d in range(members):
            out_ref[d, 0, :, rows * j : rows * (j + 1)] = whole[:, rows * d : rows * (d + 1)]


def received_kernel(keep, par, in_ref, *outs):
    members, _, rows, lanes = in_ref.shape
    group = lanes // rows
    block = in_ref[:, 0].reshape(members * rows, lanes)
    turned = block.T
    for j in range(group):
        plane = pl.program_id(0) * group + j
        lines = turned[rows * j : rows * (j + 1)]
        results = solve_lanes(lines, par, plane)
        for a, part in enumerate(results):
            outs[0][j, :, CHUNK * a : CHUNK * (a + 1)] = part
        if keep:
            outs[1][j] = lines


def stencil_kernel(adjoint, members, par, rho, rho_z, rho_y, tensor, grad, rim_z, rim_y, *rest):
    if adjoint:
        other, other_y, out_ref, cell, flux_y, flux_z, partial = rest
    else:
        out_ref, cell, flux_y, flux_z, partial = rest
    planes, rows, lanes = rho.shape
    k = pl.program_id(0)
    now = lax.rem(k, 3)
    ring = lax.rem(k, 2)

    @pl.when(k == 0)
    def _():
        flux_z[2] = rim_z[0]

    @pl.when(k == planes)
    def _():
        flux_z[now] = rim_z[1]

    @pl.when(k < planes)
    def _():
        root = par[k, 1]
        scales = (root, root, 1.0)
        cell[8 : 8 + rows] = rho[k]
        cell[7:8] = rho_y[k, 0:1]
        cell[8 + rows : 9 + rows] = rho_y[k, 1:2]
        flux_y[7:8] = rim_y[k, 0:1]
        flux_y[8 + rows : 9 + rows] = rim_y[k, 1:2]
        before = jnp.maximum(k - 1, 0)
        after = jnp.minimum(k + 1, planes - 1)
        for s in range(rows // STRIP):
            top = STRIP * s
            span = slice(top, top + STRIP)
            centre = cell[8 + top : 8 + top + STRIP]
            low = jnp.where(k == 0, rho_z[0, span], rho[before, span])
            high = jnp.where(k == planes - 1, rho_z[1, span], rho[after, span])
            vectors = [
                0.5 * (pltpu.roll(centre, lanes - 1, 1) - pltpu.roll(centre, 1, 1)),
                0.5 * (cell[9 + top : 9 + top + STRIP] - cell[7 + top : 7 + top + STRIP]),
                0.5 * (high - low),
            ]
            drift = [grad[m, 0, span].astype(jnp.float32) for m in range(3)]
            if not adjoint:
                vectors = [vectors[m] + drift[m] * centre for m in range(3)]
            scaled = [scales[m] * vectors[m] for m in range(3)]
            entry = [tensor[m, 0, span].astype(jnp.float32) for m in range(6)]
            fluxes = []
            for target in range(3):
                total = scaled[target]
                for source in range(3):
                    total = total + entry[ENTRY[target][source]] * scaled[source]
                fluxes.append(total if target == 2 else root * total)
            change = 0.5 * (pltpu.roll(fluxes[0], lanes - 1, 1) - pltpu.roll(fluxes[0], 1, 1))
            if adjoint:
                for m in range(3):
                    change = change - drift[m] * fluxes[m]
            flux_y[8 + top : 8 + top + STRIP] = fluxes[1]
            flux_z[now, span] = fluxes[2]
            partial[ring, span] = change
        for s in range(rows // STRIP):
            top = STRIP * s
            span = slice(top, top + STRIP)
            partial[ring, span] = partial[ring, span] + 0.5 * (
                flux_y[9 + top : 9 + top + STRIP] - flux_y[7 + top : 7 + top + STRIP]
            )

    @pl.when(k > 0)
    def _():
        q = k - 1
        rate = par[q, 0]
        field, field_y = (other, other_y) if adjoint else (rho, rho_y)
        change = partial[1 - ring] + 0.5 * (flux_z[now] - flux_z[lax.rem(k + 1, 3)])
        pick = (q, slice(None), slice(None))
        if adjoint:
            centre = other[0]
            edge = other_y[q]
        else:
            centre = rho[pick]
            edge = rho_y[q]
        index = lax.broadcasted_iota(jnp.int32, (rows, lanes), 0)
        above = jnp.where(index == 0, edge[0:1], pltpu.roll(centre, 1, 0))
        below = jnp.where(index == rows - 1, edge[1:2], pltpu.roll(centre, rows - 1, 0))
        level = centre - rate * (above + below - 2.0 * centre)
        if adjoint:
            out_ref[0] = level + change
        else:
            parts = solve_lanes(change, par, q)
            parts = [
                part + level[:, CHUNK * a : CHUNK * (a + 1)] for a, part in enumerate(parts)
            ]
            group = out_ref.shape[3] // rows
            pack_plane(parts, out_ref, lax.rem(q, group), members, rows)


def exchange(low_edge, high_edge, axis):
    count = lax.axis_size(axis)
    forward = [(i, (i + 1) % count) for i in range(count)]
    backward = [(target, source) for source, target in forward]
    return lax.ppermute(high_edge, axis, forward), lax.ppermute(low_edge, axis, backward)


def rim_flux(target, centre, differences, tensor, grad, root, adjoint):
    scales = (root, root, 1.0)
    total = 0.0
    for source in range(3):
        vector = 0.5 * differences[source]
        if not adjoint:
            vector = vector + grad[source].astype(jnp.float32) * centre
        entry = tensor[ENTRY[target][source]].astype(jnp.float32)
        if target == source:
            entry = entry + 1.0
        total = total + scales[target] * scales[source] * entry * vector
    return total


def ends(array, axis):
    size = array.shape[axis]
    return jnp.concatenate(
        [lax.slice_in_dim(array, 0, 1, axis=axis), lax.slice_in_dim(array, size - 1, size, axis=axis)],
        axis,
    )


def flux_rims(field, field_z, field_y, field_z_y, outer_y, coupling_y, drift_y, tensor, grad, root, adjoint):
    def across_lanes(part):
        return jnp.roll(part, -1, 2) - jnp.roll(part, 1, 2)

    plane = ends(field, 0)
    outer = ends(field_y, 0)
    above = jnp.concatenate([outer[:, :1], plane[:, :-1]], 1)
    below = jnp.concatenate([plane[:, 1:], outer[:, 1:]], 1)
    before = jnp.concatenate([field_z[:1], field[-2:-1]], 0)
    after = jnp.concatenate([field[1:2], field_z[1:]], 0)
    flux_z = rim_flux(
        2,
        plane,
        (across_lanes(plane), below - above, after - before),
        ends(tensor, 1),
        ends(grad, 1),
        ends(root, 0),
        adjoint,
    )
    z_low, z_high = exchange(flux_z[:1], flux_z[1:], "ga")
    sides = []
    for side in range(2):
        row = field_y[:, side : side + 1]
        corner = field_z_y[:, side : side + 1]
        before = jnp.concatenate([corner[:1], row[:-1]], 0)
        after = jnp.concatenate([row[1:], corner[1:]], 0)
        if side == 0:
            along = field[:, :1] - outer_y[:, :1]
        else:
            along = outer_y[:, 1:] - field[:, -1:]
        total = 0.0
        for source, difference in enumerate((across_lanes(row), along, after - before)):
            vector = 0.5 * difference
            if not adjoint:
                vector = vector + drift_y[side][:, source : source + 1] * row
            total = total + coupling_y[side][:, source : source + 1] * vector
        sides.append(total)
    return jnp.concatenate([z_low, z_high], 0), jnp.concatenate(sides, 1)


def edge_row(array, member, row):
    planes, lanes = array.shape[1], array.shape[3]
    part = lax.slice(array, (member, 0, row, 0), (member + 1, planes, row + 1, lanes))
    return part.reshape(planes, 1, lanes).astype(jnp.float32)


def edge_terms(tensor, grad, root, row):
    scales = (root, root, 1.0)
    terms = []
    for source in range(3):
        entry = edge_row(tensor, ENTRY[1][source], row)
        if source == 1:
            entry = entry + 1.0
        terms.append(root * scales[source] * entry)
    for source in range(3):
        terms.append(edge_row(grad, source, row))
    return terms


def whole_block(array):
    zeros = (0,) * array.ndim
    return pl.BlockSpec(array.shape, lambda k: zeros)


def stencil(
    adjoint, members, group, par, root, field, field_z, field_y, outer_y, coupling_y, drift_y, tensor, grad, extra=()
):
    planes, rows, lanes = field.shape
    low, high = exchange(field_y[:1], field_y[-1:], "ga")
    field_z_y = jnp.concatenate([low, high], 0)
    rim_z, rim_y = flux_rims(
        field, field_z, field_y, field_z_y, outer_y, coupling_y, drift_y, tensor, grad, root, adjoint
    )
    stream = lambda k: (0, jnp.minimum(k, planes - 1), 0, 0)
    specs = [
        pl.BlockSpec(memory_space=pltpu.SMEM),
        whole_block(field),
        whole_block(field_z),
        whole_block(field_y),
        pl.BlockSpec((6, 1, rows, lanes), stream),
        pl.BlockSpec((3, 1, rows, lanes), stream),
        whole_block(rim_z),
        whole_block(rim_y),
    ]
    args = [par, field, field_z, field_y, tensor, grad, rim_z, rim_y]
    if adjoint:
        other, other_y = extra
        specs += [
            pl.BlockSpec((1, rows, lanes), lambda k: (jnp.maximum(k - 1, 0), 0, 0)),
            whole_block(other_y),
        ]
        args += [other, other_y]
        out_shape = jax.ShapeDtypeStruct(field.shape, jnp.float32)
        out_spec = pl.BlockSpec((1, rows, lanes), lambda k: (jnp.maximum(k - 1, 0), 0, 0))
    else:
        out_shape = jax.ShapeDtypeStruct((members, planes // group, rows, group * rows), jnp.float32)
        out_spec = pl.BlockSpec(
            (members, 1, rows, group * rows), lambda k: (0, jnp.maximum(k - 1, 0) // group, 0, 0)
        )
    return pl.pallas_call(
        functools.partial(stencil_kernel, adjoint, members),
        grid=(planes + 1,),
        out_shape=out_shape,
        in_specs=specs,
        out_specs=out_spec,
        scratch_shapes=[
            pltpu.VMEM((rows + 16, lanes), jnp.float32),
            pltpu.VMEM((rows + 16, lanes), jnp.float32),
            pltpu.VMEM((3, rows, lanes), jnp.float32),
            pltpu.VMEM((2, rows, lanes), jnp.float32),
        ],
        compiler_params=pltpu.CompilerParams(vmem_limit_bytes=LIMIT),
        cost_estimate=pl.CostEstimate(
            flops=80 * field.size, bytes_accessed=32 * field.size, transcendentals=0
        ),
    )(*args)


def lines_solved(members, group, par, field):
    planes, rows, lanes = field.shape
    return pl.pallas_call(
        functools.partial(lines_kernel, members),
        grid=(planes // group,),
        out_shape=jax.ShapeDtypeStruct(
            (members, planes // group, rows, group * rows), jnp.float32
        ),
        in_specs=[
            pl.BlockSpec(memory_space=pltpu.SMEM),
            pl.BlockSpec((group, rows, lanes), lambda k: (k, 0, 0)),
        ],
        out_specs=pl.BlockSpec((members, 1, rows, group * rows), lambda k: (0, k, 0, 0)),
        compiler_params=pltpu.CompilerParams(vmem_limit_bytes=LIMIT),
        cost_estimate=pl.CostEstimate(
            flops=3072 * field.size, bytes_accessed=8 * field.size, transcendentals=0
        ),
    )(par, field)


def received_solved(keep, par, block):
    members, groups, rows, packed = block.shape
    group = packed // rows
    shape = jax.ShapeDtypeStruct((groups * group, rows, members * rows), jnp.float32)
    spec = pl.BlockSpec((group, rows, members * rows), lambda k: (k, 0, 0))
    return pl.pallas_call(
        functools.partial(received_kernel, keep),
        grid=(groups,),
        out_shape=[shape, shape] if keep else [shape],
        in_specs=[
            pl.BlockSpec(memory_space=pltpu.SMEM),
            pl.BlockSpec((members, 1, rows, packed), lambda k: (0, k, 0, 0)),
        ],
        out_specs=[spec, spec] if keep else [spec],
        compiler_params=pltpu.CompilerParams(vmem_limit_bytes=LIMIT),
        cost_estimate=pl.CostEstimate(
            flops=3072 * block.size, bytes_accessed=8 * block.size, transcendentals=0
        ),
    )(par, block)


def traded(block):
    return lax.all_to_all(block, ("gx", "gy"), split_axis=0, concat_axis=0, tiled=True)


def local(density, tensor, grad_u, plane_rate, cotangent):
    planes, rows, lanes = density.shape
    members = lanes // rows
    group = 128 // math.gcd(rows, 128)
    if rows % STRIP or planes % group or lanes % CHUNK:
        return local_general(density, tensor, grad_u, plane_rate, cotangent)
    root = jnp.sqrt(plane_rate)
    half = 0.5 / root
    theta = 2.0 * jnp.log1p(half + half * half / (1.0 + jnp.sqrt(1.0 + half * half)))
    kappa = 1.0 / jnp.sqrt(1.0 + 4.0 * plane_rate)
    wrap = 1.0 / (1.0 - jnp.exp(-theta * lanes))
    step = jnp.exp(-theta * CHUNK)
    par = jnp.stack([plane_rate, root, theta, kappa, wrap, step], 1)
    root = root[:, None, None]
    low, high = exchange(
        jnp.concatenate([density[:, :2]] + edge_terms(tensor, grad_u, root, 0), 1),
        jnp.concatenate([density[:, -2:]] + edge_terms(tensor, grad_u, root, rows - 1), 1),
        ("gx", "gy"),
    )
    swept = lines_solved(members, group, par, cotangent)
    z_low, z_high = exchange(density[:1], density[-1:], "ga")
    swept, low, high, z_low, z_high = lax.optimization_barrier((swept, low, high, z_low, z_high))
    swept = traded(swept)
    coupling_y = (low[:, 2:5], high[:, 2:5])
    drift_y = (low[:, 5:8], high[:, 5:8])
    packed = stencil(
        False,
        members,
        group,
        par,
        root,
        density,
        jnp.concatenate([z_low, z_high], 0),
        jnp.concatenate([low[:, 1:2], high[:, :1]], 1),
        jnp.concatenate([low[:, :1], high[:, 1:2]], 1),
        coupling_y,
        drift_y,
        tensor,
        grad_u,
    )
    packed, swept = lax.optimization_barrier((packed, swept))
    settled, returned = received_solved(True, par, swept)
    low, high = exchange(
        jnp.concatenate([settled[:, :2], returned[:, :1]], 1),
        jnp.concatenate([settled[:, -2:], returned[:, -1:]], 1),
        ("gx", "gy"),
    )
    z_low, z_high = exchange(settled[:1], settled[-1:], "ga")
    packed, low, high, z_low, z_high = lax.optimization_barrier((packed, low, high, z_low, z_high))
    moved = traded(packed)
    adjoint_density = stencil(
        True,
        members,
        group,
        par,
        root,
        settled,
        jnp.concatenate([z_low, z_high], 0),
        jnp.concatenate([low[:, 1:2], high[:, :1]], 1),
        jnp.concatenate([low[:, :1], high[:, 1:2]], 1),
        coupling_y,
        drift_y,
        tensor,
        grad_u,
        (returned, jnp.concatenate([low[:, 2:], high[:, 2:]], 1)),
    )
    moved, adjoint_density = lax.optimization_barrier((moved, adjoint_density))
    (new_density,) = received_solved(False, par, moved)
    return (new_density, adjoint_density)


def solution(mesh):
    placed = (
        P("ga", ("gx", "gy"), None),
        P(None, "ga", ("gx", "gy"), None),
        P(None, "ga", ("gx", "gy"), None),
        P("ga"),
        P("ga", ("gx", "gy"), None),
    )
    return jax.shard_map(
        local,
        mesh=mesh,
        in_specs=placed,
        out_specs=(P("ga", ("gx", "gy"), None), P("ga", ("gx", "gy"), None)),
        check_vma=False,
    )
```
